32 devices in a mesh: parts: 2 (over x), dp: 2 (over core), mp: 8 (over z, y).
Axes of the slice: x: 2, y: 2, z: 4, core: 2. Of those that a mesh axis runs over, the one named last changes fastest.
Arguments:
- patches: bfloat16 [1024, 6144], P(('parts', 'dp', 'mp')), parts along dimension 0, may hold values from -6 to 6
- norm_gain: float32 [6144], replicated, may hold values from 0.1 to 1.9
- query_gain: float32 [128], replicated, may hold values from 0.5 to 9
- key_gain: float32 [128], replicated, may hold values from 0.5 to 9
- joined_in: bfloat16 [6144, 16, 1536], P(None, ('dp', 'mp')), may hold values from -0.078125 to 0.078125
- joined_out: bfloat16 [16, 1024, 6144], P(('dp', 'mp')), may hold values from -0.046875 to 0.046875
Outputs:
- layer_out: bfloat16 [1024, 6144], P(('parts', 'dp', 'mp')), parts along dimension 0
The draws below stay inside these ranges and needn't reach their ends.
There are 2 independent parts, one for each index of `parts`. The reference program is written for one: setup_inputs(seed, part) draws one part's arguments, and reference() takes and returns one part's arrays. A program takes and returns all parts, laid end to end along the dimension named above; an argument that names none is the same for every part. Nothing has to cross between parts.
All inputs are finite; a program needn't handle non-finite values.
Results may differ from the reference program's by a relative error of at most 0.012.
The reference program's roundings to bfloat16 on the way (of `normed`, `values`, `weights`, `attended`, `activated` and `mixed`) count: a program that leaves them out, or rounds other values in their place, can miss the bound.
Values may be sent and summed in bfloat16 or wider, within the bound.
A program may use at most 128 MiB of HBM per device.

```python
import jax
import jax.numpy as jnp
from jax import lax

D = 6144
HD = 128
HEADS = 32
FF = 12288
PATCH = 256
BLOCKS = 16
BW = 1536
BW2 = 1024
TOKENS = 512


def draw_query_gain(key, part):
    key = jax.random.fold_in(key, 11)
    return jnp.exp(jax.random.uniform(key, (HD,), jnp.float32, -0.69, 0.69))


def draw_key_gain(key, part):
    key = jax.random.fold_in(key, 23)
    return jnp.exp(jax.random.uniform(key, (HD,), jnp.float32, -0.69, 0.69))


def steps_of(stream_key, shape, pieces, least, high):
    level = 1.0
    for axis_at, blocks in pieces:
        steps = jax.random.uniform(jax.random.fold_in(jax.random.fold_in(stream_key, 6), axis_at), (blocks,), jnp.float32, least / len(pieces), high / len(pieces))
        level = level * jnp.repeat(jnp.exp(steps), shape[axis_at] // blocks).reshape((-1,) + (1,) * (len(shape) - 1 - axis_at))
    return level


def bell_draw(key, shape, deviation, limit, cuts=(), held_as=jnp.bfloat16):
    drawn = jax.random.normal(key, shape, jnp.float32) * deviation
    if len(cuts) > 0:
        drawn = steps_of(key, shape, cuts, -0.22, 0.18) * drawn
    return jnp.clip(drawn, min=-limit, max=limit).astype(held_as)


def setup_inputs(seed: int = 0, part: int = 0) -> dict:
    key_list = jax.random.split(jax.random.key(seed), 7)
    own_keys = jax.random.split(jax.random.fold_in(key_list[6], part), 7)
    return {
        "patches": bell_draw(own_keys[0], (TOKENS, D), 1.0, 6.0, ((0, 16),)),
        "norm_gain": jnp.clip(1.0 + 0.18 * jax.random.normal(key_list[1], (D,), jnp.float32), 0.1, 1.9),
        "query_gain": draw_query_gain(jax.random.fold_in(key_list[6], 71), part),
        "key_gain": draw_key_gain(jax.random.fold_in(key_list[6], 71), part),
        "joined_in": bell_draw(key_list[4], (D, BLOCKS, BW), D ** -0.5, 0.078125, ((1, 16),)),
        "joined_out": bell_draw(key_list[5], (BLOCKS, BW2, D), (HEADS * HD + FF) ** -0.5, 0.046875, ((0, 16),)),
    }


def normalize(source, gain):
    values = source.astype(jnp.float32)
    center = values - lax.optimization_barrier(jnp.mean(values, axis=-1, keepdims=True))
    spread = lax.optimization_barrier(jnp.mean(center * center, axis=-1, keepdims=True))
    return (center * lax.rsqrt(spread + 1e-06) * gain).astype(jnp.bfloat16)

def attend(joined, query_gain, key_gain, width_att):
    row_count, block_count, _ = joined.shape
    head_dim = query_gain.shape[0]
    heads = block_count * width_att // head_dim
    images = row_count // PATCH
    queries = normalize(joined[:, :, :width_att].reshape(row_count, heads, head_dim), query_gain)
    keys = normalize(joined[:, :, width_att:2 * width_att].reshape(row_count, heads, head_dim), key_gain)
    values = joined[:, :, 2 * width_att:3 * width_att].reshape(row_count, heads, head_dim).astype(jnp.bfloat16)
    queries = queries.reshape(images, PATCH, heads, head_dim).astype(jnp.float32)
    keys = keys.reshape(images, PATCH, heads, head_dim).astype(jnp.float32)
    values = values.reshape(images, PATCH, heads, head_dim).astype(jnp.float32)
    scores = jnp.einsum('iqhd,ikhd->ihqk', queries, keys) * head_dim ** (-0.5)
    largest = lax.optimization_barrier(jnp.max(scores, axis=-1, keepdims=True))
    raised = jnp.exp(scores - largest)
    weights = (raised / lax.optimization_barrier(jnp.sum(raised, axis=-1, keepdims=True))).astype(jnp.bfloat16)
    attended = jnp.einsum('ihqk,ikhd->iqhd', weights.astype(jnp.float32), values)
    attended = attended.astype(jnp.bfloat16).reshape(row_count, block_count, width_att)
    activated = jax.nn.gelu(joined[:, :, 3 * width_att:], approximate=False).astype(jnp.bfloat16)
    return jnp.concatenate([attended, activated], axis=2)

def reference(patches, norm_gain, query_gain, key_gain, joined_in, joined_out):
    width_mix = joined_out.shape[1]
    width_att = (joined_in.shape[2] - width_mix) // 2
    normed = normalize(patches, norm_gain)
    joined = jnp.dot(normed, joined_in.reshape(joined_in.shape[0], -1), preferred_element_type=jnp.float32)
    joined = joined.reshape(joined.shape[0], joined_in.shape[1], joined_in.shape[2])
    mixed = attend(joined, query_gain, key_gain, width_att)
    flat = mixed.reshape(mixed.shape[0], -1)
    branch = jnp.dot(flat, joined_out.reshape(-1, joined_out.shape[2]), preferred_element_type=jnp.float32)
    return (patches.astype(jnp.float32) + branch).astype(jnp.bfloat16)
```

```python
import functools

import jax
import jax.numpy as jnp
from jax import lax
from jax.experimental import pallas as pl
from jax.experimental.pallas import tpu as pltpu
from jax.sharding import PartitionSpec as P

PATCH = 256
MESH = pl.DeviceIdType.MESH
Y = 2


def normalize(values, gain):
    center = values - jnp.mean(values, axis=-1, keepdims=True)
    spread = jnp.mean(center * center, axis=-1, keepdims=True)
    return (center * lax.rsqrt(spread + 1e-06) * gain).astype(jnp.bfloat16)


def dot(a, b):
    return jnp.dot(a, b, preferred_element_type=jnp.float32)


def weave(first, second):
    tagged = [((i + 0.5) / len(first), 0, f) for i, f in enumerate(first)]
    tagged += [((i + 0.5) / len(second), 1, f) for i, f in enumerate(second)]
    return [f for _, _, f in sorted(tagged, key=lambda t: t[:2])]


def kernel(
    M, patches, norm_gain, query_gain, key_gain, win_hbm, wout_hbm, out,
    win, wout, xg, joined, mixed, snd, rsib, S, Ry, RZ, fsnd, frecv,
    w_sem, sa_s, sa_r, az_s, az_r, ay_s, ay_r, as_s, as_r,
    ps_s, ps_r, ry_s, ry_r, rz_s, rz_r, f_s, f_r,
):
    R, D = patches.shape
    H = D // 2
    Z = M // Y
    G = M * R
    BW = win.shape[1]
    BW2 = wout.shape[1]
    HD = query_gain.shape[1]
    ATT = (BW - BW2) // 2
    heads = ATT // HD
    NC = snd.shape[1]
    CW = snd.shape[3]
    c = lax.axis_index("dp")
    o = 1 - c
    me = lax.axis_index("mp")
    z = me // Y
    y = me % Y
    yn = z * Y + 1 - y
    drains = []

    def remote(src, dst, ssem, rsem, dev):
        return pltpu.make_async_remote_copy(
            src_ref=src, dst_ref=dst, send_sem=ssem, recv_sem=rsem, device_id=dev, device_id_type=MESH
        )

    def send(cond, make):
        if cond is None:
            make().start()
        else:
            pl.when(cond)(lambda: make().start())
        drains.append((cond, make))

    wcopies = []
    step = D // 4
    for i in range(4):
        wcopies.append(pltpu.make_async_copy(win_hbm.at[pl.ds(i * step, step)], win.at[pl.ds(i * step, step)], w_sem.at[i]))
    for i in range(2):
        wcopies.append(pltpu.make_async_copy(wout_hbm.at[:, pl.ds(i * H, H)], wout.at[i], w_sem.at[4 + i]))
    for w in wcopies:
        w.start()

    barrier = pltpu.get_barrier_semaphore()
    pl.semaphore_signal(barrier, inc=1, device_id={"dp": o}, device_id_type=MESH)
    pl.semaphore_signal(barrier, inc=1, device_id={"mp": yn}, device_id_type=MESH)
    has_dn = z > 0
    has_up = z < Z - 1

    @pl.when(has_dn)
    def _():
        pl.semaphore_signal(barrier, inc=1, device_id={"mp": me - Y}, device_id_type=MESH)

    @pl.when(has_up)
    def _():
        pl.semaphore_signal(barrier, inc=1, device_id={"mp": me + Y}, device_id_type=MESH)

    normed = normalize(patches[...].astype(jnp.float32), norm_gain[...])
    xg[0, c, me] = normed[:, :H]
    xg[1, c, me] = normed[:, H:]
    pl.semaphore_wait(barrier, 2 + (z > 0).astype(jnp.int32) + (z < Z - 1).astype(jnp.int32))

    def own_to_sibling(h):
        return remote(xg.at[h, c, me], xg.at[h, c, me], sa_s.at[h], sa_r.at[h], {"dp": o})

    def own_from_sibling(h):
        return remote(xg.at[h, o, me], xg.at[h, o, me], sa_s.at[h], sa_r.at[h], {"dp": o})

    send(None, lambda: own_to_sibling(o))
    send(None, lambda: own_to_sibling(c))

    def zcopy(g, d, k, b):
        to = me + Y if d == 0 else me - Y
        return remote(xg.at[c, g, b], xg.at[c, g, b], az_s.at[g, d, k], az_r.at[g, d, k], {"mp": to})

    def ycopy(g, zb, b):
        return remote(xg.at[c, g, b], xg.at[c, g, b], ay_s.at[g, zb], ay_r.at[g, zb], {"mp": yn})

    def scopy(g, h, b):
        return remote(xg.at[h, g, b], xg.at[h, g, b], as_s.at[g, b], as_r.at[g, b], {"dp": o})

    def gather_tasks(g):
        tasks = []

        def start():
            @pl.when(c != g)
            def _():
                own_from_sibling(c).wait_recv()
            send(has_up, lambda: zcopy(g, 0, 0, me))
            send(has_dn, lambda: zcopy(g, 1, 0, me))
            send(None, lambda: ycopy(g, z, me))

        tasks.append(start)

        def z_arrival(d, k):
            zb = z - k if d == 0 else z + k
            b = zb * Y + y
            here = z >= k if d == 0 else z + k < Z
            more = jnp.logical_and(here, has_up if d == 0 else has_dn)
            pl.when(here)(lambda: zcopy(g, d, k - 1, b).wait_recv())
            if k < Z - 1:
                send(more, lambda: zcopy(g, d, k, b))
            send(here, lambda: ycopy(g, zb, b))
            send(here, lambda: scopy(g, c, b))

        def y_arrival(d, k):
            zb = z - k if d == 0 else z + k
            b = zb * Y + 1 - y
            here = None if k == 0 else (z >= k if d == 0 else z + k < Z)
            if here is None:
                ycopy(g, zb, b).wait_recv()
            else:
                pl.when(here)(lambda: ycopy(g, zb, b).wait_recv())
            send(here, lambda: scopy(g, c, b))

        for k in range(1, Z):
            for d in (0, 1):
                tasks.append(functools.partial(z_arrival, d, k))
            if k == 1:
                tasks.append(functools.partial(y_arrival, 0, 0))
            else:
                for d in (0, 1):
                    tasks.append(functools.partial(y_arrival, d, k - 1))
        for d in (0, 1):
            tasks.append(functools.partial(y_arrival, d, Z - 1))

        def finish():
            @pl.when(c != g)
            def _():
                own_from_sibling(o).wait_recv()

            @pl.loop(0, M)
            def _(b):
                @pl.when(b != me)
                def _():
                    scopy(g, o, b).wait_recv()

        tasks.append(finish)
        return tasks

    def flat(ref):
        return ref[...].reshape(G, ref.shape[-1])

    NW = 256

    def project(g, first, last):
        @pl.loop(first, last)
        def _(n):
            columns = pl.ds(pl.multiple_of(n * NW, NW), NW)
            left = dot(flat(xg.at[0, g]), win[pl.ds(0, H), columns])
            joined[:, columns] = left + dot(flat(xg.at[1, g]), win[pl.ds(H, H), columns])

    def attention(i, h):
        rows = pl.ds(i * PATCH, PATCH)
        part = lambda at: joined[rows, pl.ds(at * ATT + h * HD, HD)]
        q = normalize(part(0), query_gain[...])
        k = normalize(part(1), key_gain[...])
        v = part(2).astype(jnp.bfloat16)
        scores = lax.dot_general(
            q, k, (((1,), (1,)), ((), ())), preferred_element_type=jnp.float32
        ) * HD ** (-0.5)
        raised = jnp.exp(scores - jnp.max(scores, axis=-1, keepdims=True))
        weights = (raised / jnp.sum(raised, axis=-1, keepdims=True)).astype(jnp.bfloat16)
        mixed[rows, pl.ds(h * HD, HD)] = dot(weights, v).astype(jnp.bfloat16)

    def gelu(n):
        x = joined[:, pl.ds(3 * ATT + n * HD, HD)]
        mixed[:, pl.ds(ATT + n * HD, HD)] = (0.5 * x * (1.0 + lax.erf(x * 0.5**0.5))).astype(jnp.bfloat16)

    def psend(g, n):
        return remote(snd.at[g, n], rsib.at[g, n], ps_s.at[g, n], ps_r.at[g, n], {"dp": o})

    def back_other(g):
        @pl.loop(0, NC)
        def _(n):
            columns = pl.ds(pl.multiple_of(n * CW, CW), CW)
            snd[g, n] = dot(mixed[...], wout[o, :, columns]).astype(jnp.bfloat16)
            psend(g, n).start()

    def back_own(g):
        @pl.loop(0, NC)
        def _(n):
            columns = pl.ds(pl.multiple_of(n * CW, CW), CW)
            term = dot(mixed[...], wout[c, :, columns])
            psend(g, n).wait()
            total = (term + rsib[g, n].astype(jnp.float32)).astype(jnp.bfloat16)
            S[g, :, :, columns] = total.reshape(M, R, CW)

    def compute_tasks(g):
        tasks = []
        chunks = BW // NW
        per = max(1, chunks // 3)
        for a in range(0, chunks, per):
            tasks.append(functools.partial(project, g, a, min(chunks, a + per)))
        for i in range(G // PATCH):
            for h in range(heads):
                tasks.append(functools.partial(attention, i, h))
        units = (BW2 - ATT) // HD
        for n in range(units):
            tasks.append(functools.partial(gelu, n))
        tasks.append(functools.partial(back_other, g))
        tasks.append(functools.partial(back_own, g))
        return tasks

    def ysum(g, zb, b):
        return remote(S.at[g, b], Ry.at[g, zb], ry_s.at[g, zb], ry_r.at[g, zb], {"mp": yn})

    def zsum(g, d, zb):
        to = me + Y if d == 0 else me - Y
        slot = zb if d == 0 else jnp.where(to // Y == zb, Z, zb)
        return remote(S.at[g, zb * Y + y], RZ.at[g, slot], rz_s.at[g, d, zb], rz_r.at[g, d, zb], {"mp": to})

    def zgot(g, d, zb, slot):
        to = me + Y if d == 0 else me - Y
        return remote(RZ.at[g, slot], RZ.at[g, slot], rz_s.at[g, d, zb], rz_r.at[g, d, zb], {"mp": to})

    def scatter_tasks(g):
        tasks = []

        def start():
            order = []
            for j in range((Z + 1) // 2):
                order += [Z - 1 - j] + ([j] if j != Z - 1 - j else [])
            for zb in order:
                send(None, functools.partial(ysum, g, zb, zb * Y + 1 - y))

        tasks.append(start)

        def pass_on(d, j):
            zb = Z - 1 - j if d == 0 else j
            here = zb > z if d == 0 else zb < z
            inner = has_dn if d == 0 else has_up

            @pl.when(here)
            def _():
                at = zb * Y + y
                ysum(g, zb, at).wait_recv()

                @pl.when(inner)
                def _():
                    zgot(g, d, zb, zb).wait_recv()
                    t = S[g, at].astype(jnp.float32) + Ry[g, zb].astype(jnp.float32)
                    S[g, at] = (t + RZ[g, zb].astype(jnp.float32)).astype(jnp.bfloat16)

                @pl.when(jnp.logical_not(inner))
                def _():
                    t = S[g, at].astype(jnp.float32) + Ry[g, zb].astype(jnp.float32)
                    S[g, at] = t.astype(jnp.bfloat16)

            send(here, functools.partial(zsum, g, d, zb))

        for j in range(Z - 1):
            for d in (0, 1):
                tasks.append(functools.partial(pass_on, d, j))

        def finish():
            ysum(g, z, me).wait_recv()
            fsnd[g] = S[g, me].astype(jnp.float32) + Ry[g, z].astype(jnp.float32)

            @pl.when(has_dn)
            def _():
                zgot(g, 0, z, z).wait_recv()
                fsnd[g] += RZ[g, z].astype(jnp.float32)

            @pl.when(has_up)
            def _():
                zgot(g, 1, z, Z).wait_recv()
                fsnd[g] += RZ[g, Z].astype(jnp.float32)

            @pl.when(c == g)
            def _():
                columns = pl.ds(pl.multiple_of(c * H, H), H)
                out[:, columns] = (patches[:, columns].astype(jnp.float32) + fsnd[g]).astype(jnp.bfloat16)

            send(c != g, lambda: remote(fsnd.at[g], frecv, f_s, f_r, {"dp": o}))

        tasks.append(finish)
        return tasks

    def run(tasks):
        for t in tasks:
            t()

    run(gather_tasks(0))
    for w in wcopies:
        w.wait()
    run(weave(gather_tasks(1), compute_tasks(0)))
    run(weave(scatter_tasks(0), compute_tasks(1)))
    run(scatter_tasks(1))
    remote(fsnd.at[0], frecv, f_s, f_r, {"dp": o}).wait_recv()
    columns = pl.ds(pl.multiple_of(o * H, H), H)
    out[:, columns] = (patches[:, columns].astype(jnp.float32) + frecv[...]).astype(jnp.bfloat16)
    for cond, make in drains:
        if cond is None:
            make().wait_send()
        else:
            pl.when(cond)(lambda make=make: make().wait_send())


def shards(M, patches, norm_gain, query_gain, key_gain, joined_in, joined_out):
    R, D = patches.shape
    H = D // 2
    Z = M // Y
    G = M * R
    BW = joined_in.shape[2]
    BW2 = joined_out.shape[1]
    CW = 512
    NC = H // CW
    bf, f32 = jnp.bfloat16, jnp.float32
    V = pl.BlockSpec(memory_space=pltpu.VMEM)
    A = pl.BlockSpec(memory_space=pl.ANY)
    dma = pltpu.SemaphoreType.DMA
    return pl.pallas_call(
        functools.partial(kernel, M),
        out_shape=jax.ShapeDtypeStruct((R, D), bf),
        in_specs=[V, V, V, V, A, A],
        out_specs=V,
        scratch_shapes=[
            pltpu.VMEM((D, BW), bf),
            pltpu.VMEM((2, BW2, H), bf),
            pltpu.VMEM((2, 2, M, R, H), bf),
            pltpu.VMEM((G, BW), f32),
            pltpu.VMEM((G, BW2), bf),
            pltpu.VMEM((2, NC, G, CW), bf),
            pltpu.VMEM((2, NC, G, CW), bf),
            pltpu.VMEM((2, M, R, H), bf),
            pltpu.VMEM((2, Z, R, H), bf),
            pltpu.VMEM((2, Z + 1, R, H), bf),
            pltpu.VMEM((2, R, H), f32),
            pltpu.VMEM((R, H), f32),
            dma((6,)),
            dma((2,)), dma((2,)),
            dma((2, 2, Z)), dma((2, 2, Z)),
            dma((2, Z)), dma((2, Z)),
            dma((2, M)), dma((2, M)),
            dma((2, NC)), dma((2, NC)),
            dma((2, Z)), dma((2, Z)),
            dma((2, 2, Z)), dma((2, 2, Z)),
            dma, dma,
        ],
        compiler_params=pltpu.CompilerParams(
            collective_id=0, has_side_effects=True, vmem_limit_bytes=63 * 1024 * 1024
        ),
        cost_estimate=pl.CostEstimate(
            flops=4 * G * D * (BW + BW2), bytes_accessed=2 * D * (BW + BW2), transcendentals=0
        ),
    )(
        patches,
        norm_gain.reshape(1, -1),
        query_gain.reshape(1, -1),
        key_gain.reshape(1, -1),
        joined_in.reshape(D, BW),
        joined_out.reshape(BW2, D),
    )


def solution(mesh):
    in_specs = (
        P(("parts", "dp", "mp"), None),
        P(),
        P(),
        P(),
        P(None, ("dp", "mp"), None),
        P(("dp", "mp"), None, None),
    )
    out_specs = P(("parts", "dp", "mp"), None)
    body = functools.partial(shards, mesh.shape["mp"])
    return jax.shard_map(body, mesh=mesh, in_specs=in_specs, out_specs=out_specs, check_vma=False)
```

```python
import functools

import jax
import jax.numpy as jnp
from jax import lax
from jax.experimental import pallas as pl
from jax.experimental.pallas import tpu as pltpu
from jax.sharding import PartitionSpec as P

PATCH = 256
FLIGHT = 2
MESH = pl.DeviceIdType.MESH
Y = 2


def normalize(values, gain):
    center = values - jnp.mean(values, axis=-1, keepdims=True)
    spread = jnp.mean(center * center, axis=-1, keepdims=True)
    return (center * lax.rsqrt(spread + 1e-06) * gain).astype(jnp.bfloat16)


def dot(a, b):
    return jnp.dot(a, b, preferred_element_type=jnp.float32)


def weave(first, second):
    tagged = [((i + 0.5) / len(first), 0, f) for i, f in enumerate(first)]
    tagged += [((i + 0.5) / len(second), 1, f) for i, f in enumerate(second)]
    return [f for _, _, f in sorted(tagged, key=lambda t: t[:2])]


def kernel(
    M, patches, norm_gain, query_gain, key_gain, win_hbm, wout_hbm, out,
    win, wout, xg, joined, mixed, snd, rsib, S, Ry, RZ, fsnd, frecv,
    w_sem, sa_s, sa_r, az_s, az_r, ay_s, ay_r, as_s, as_r,
    ps_s, ps_r, ry_s, ry_r, rz_s, rz_r, f_s, f_r,
):
    R, D = patches.shape
    H = D // 2
    Z = M // Y
    G = M * R
    BW = win.shape[1]
    BW2 = wout.shape[1]
    HD = query_gain.shape[1]
    ATT = (BW - BW2) // 2
    heads = ATT // HD
    NC = snd.shape[1]
    CW = snd.shape[3]
    c = lax.axis_index("dp")
    o = 1 - c
    me = lax.axis_index("mp")
    z = me // Y
    y = me % Y
    yn = z * Y + 1 - y
    drains = []

    def remote(src, dst, ssem, rsem, dev):
        return pltpu.make_async_remote_copy(
            src_ref=src, dst_ref=dst, send_sem=ssem, recv_sem=rsem, device_id=dev, device_id_type=MESH
        )

    def send(cond, make):
        if cond is None:
            make().start()
        else:
            pl.when(cond)(lambda: make().start())
        drains.append((cond, make))

    wcopies = []
    step = D // 4
    for i in range(4):
        wcopies.append(pltpu.make_async_copy(win_hbm.at[pl.ds(i * step, step)], win.at[pl.ds(i * step, step)], w_sem.at[i]))
    for i in range(2):
        wcopies.append(pltpu.make_async_copy(wout_hbm.at[:, pl.ds(i * H, H)], wout.at[i], w_sem.at[4 + i]))
    for w in wcopies:
        w.start()

    barrier = pltpu.get_barrier_semaphore()
    pl.semaphore_signal(barrier, inc=1, device_id={"dp": o}, device_id_type=MESH)
    pl.semaphore_signal(barrier, inc=1, device_id={"mp": yn}, device_id_type=MESH)
    has_dn = z > 0
    has_up = z < Z - 1

    @pl.when(has_dn)
    def _():
        pl.semaphore_signal(barrier, inc=1, device_id={"mp": me - Y}, device_id_type=MESH)

    @pl.when(has_up)
    def _():
        pl.semaphore_signal(barrier, inc=1, device_id={"mp": me + Y}, device_id_type=MESH)

    normed = normalize(patches[...].astype(jnp.float32), norm_gain[...])
    xg[0, c, me] = normed[:, :H]
    xg[1, c, me] = normed[:, H:]
    pl.semaphore_wait(barrier, 2 + (z > 0).astype(jnp.int32) + (z < Z - 1).astype(jnp.int32))

    def own_to_sibling(h):
        return remote(xg.at[h, c, me], xg.at[h, c, me], sa_s.at[h], sa_r.at[h], {"dp": o})

    def own_from_sibling(h):
        return remote(xg.at[h, o, me], xg.at[h, o, me], sa_s.at[h], sa_r.at[h], {"dp": o})

    send(None, lambda: own_to_sibling(o))
    send(None, lambda: own_to_sibling(c))

    def zcopy(g, d, k, b):
        to = me + Y if d == 0 else me - Y
        return remote(xg.at[c, g, b], xg.at[c, g, b], az_s.at[g, d, k], az_r.at[g, d, k], {"mp": to})

    def ycopy(g, zb, b):
        return remote(xg.at[c, g, b], xg.at[c, g, b], ay_s.at[g, zb], ay_r.at[g, zb], {"mp": yn})

    def scopy(g, h, b):
        return remote(xg.at[h, g, b], xg.at[h, g, b], as_s.at[g, b], as_r.at[g, b], {"dp": o})

    def gather_tasks(g):
        tasks = []

        def start():
            @pl.when(c != g)
            def _():
                own_from_sibling(c).wait_recv()
            send(has_up, lambda: zcopy(g, 0, 0, me))
            send(has_dn, lambda: zcopy(g, 1, 0, me))
            send(None, lambda: ycopy(g, z, me))

        tasks.append(start)

        def z_arrival(d, k):
            zb = z - k if d == 0 else z + k
            b = zb * Y + y
            here = z >= k if d == 0 else z + k < Z
            more = jnp.logical_and(here, has_up if d == 0 else has_dn)
            pl.when(here)(lambda: zcopy(g, d, k - 1, b).wait_recv())
            if k < Z - 1:
                send(more, lambda: zcopy(g, d, k, b))
            send(here, lambda: ycopy(g, zb, b))
            send(here, lambda: scopy(g, c, b))

        def y_arrival(d, k):
            zb = z - k if d == 0 else z + k
            b = zb * Y + 1 - y
            here = None if k == 0 else (z >= k if d == 0 else z + k < Z)
            if here is None:
                ycopy(g, zb, b).wait_recv()
            else:
                pl.when(here)(lambda: ycopy(g, zb, b).wait_recv())
            send(here, lambda: scopy(g, c, b))

        for k in range(1, Z):
            for d in (0, 1):
                tasks.append(functools.partial(z_arrival, d, k))
            if k == 1:
                tasks.append(functools.partial(y_arrival, 0, 0))
            else:
                for d in (0, 1):
                    tasks.append(functools.partial(y_arrival, d, k - 1))
        for d in (0, 1):
            tasks.append(functools.partial(y_arrival, d, Z - 1))

        def finish():
            @pl.when(c != g)
            def _():
                own_from_sibling(o).wait_recv()

            @pl.loop(0, M)
            def _(b):
                @pl.when(b != me)
                def _():
                    scopy(g, o, b).wait_recv()

        tasks.append(finish)
        return tasks

    def flat(ref):
        return ref[...].reshape(G, ref.shape[-1])

    NW = 256

    def project(g, first, last):
        @pl.loop(first, last)
        def _(n):
            columns = pl.ds(pl.multiple_of(n * NW, NW), NW)
            left = dot(flat(xg.at[0, g]), win[pl.ds(0, H), columns])
            joined[:, columns] = left + dot(flat(xg.at[1, g]), win[pl.ds(H, H), columns])

    def attention(i, h):
        rows = pl.ds(i * PATCH, PATCH)
        part = lambda at: joined[rows, pl.ds(at * ATT + h * HD, HD)]
        q = normalize(part(0), query_gain[...])
        k = normalize(part(1), key_gain[...])
        v = part(2).astype(jnp.bfloat16)
        scores = lax.dot_general(
            q, k, (((1,), (1,)), ((), ())), preferred_element_type=jnp.float32
        ) * HD ** (-0.5)
        raised = jnp.exp(scores - jnp.max(scores, axis=-1, keepdims=True))
        weights = (raised / jnp.sum(raised, axis=-1, keepdims=True)).astype(jnp.bfloat16)
        mixed[rows, pl.ds(h * HD, HD)] = dot(weights, v).astype(jnp.bfloat16)

    def gelu(n):
        x = joined[:, pl.ds(3 * ATT + n * HD, HD)]
        mixed[:, pl.ds(ATT + n * HD, HD)] = (0.5 * x * (1.0 + lax.erf(x * 0.5**0.5))).astype(jnp.bfloat16)

    def psend(g, n):
        return remote(snd.at[g, n], rsib.at[g, n], ps_s.at[g, n], ps_r.at[g, n], {"dp": o})

    def back_other(g):
        @pl.loop(0, NC)
        def _(n):
            columns = pl.ds(pl.multiple_of(n * CW, CW), CW)
            snd[g, n] = dot(mixed[...], wout[o, :, columns]).astype(jnp.bfloat16)
            psend(g, n).start()

    def back_own(g):
        @pl.loop(0, NC)
        def _(n):
            columns = pl.ds(pl.multiple_of(n * CW, CW), CW)
            term = dot(mixed[...], wout[c, :, columns])
            psend(g, n).wait()
            total = (term + rsib[g, n].astype(jnp.float32)).astype(jnp.bfloat16)
            S[g, :, :, columns] = total.reshape(M, R, CW)

    def compute_tasks(g):
        tasks = []
        chunks = BW // NW
        per = max(1, chunks // 3)
        for a in range(0, chunks, per):
            tasks.append(functools.partial(project, g, a, min(chunks, a + per)))
        for i in range(G // PATCH):
            for h in range(heads):
                tasks.append(functools.partial(attention, i, h))
        units = (BW2 - ATT) // HD
        for n in range(units):
            tasks.append(functools.partial(gelu, n))
        tasks.append(functools.partial(back_other, g))
        tasks.append(functools.partial(back_own, g))
        return tasks

    def ysum(g, zb, b):
        return remote(S.at[g, b], Ry.at[g, zb], ry_s.at[g, zb], ry_r.at[g, zb], {"mp": yn})

    def zsum(g, d, zb):
        to = me + Y if d == 0 else me - Y
        slot = zb if d == 0 else jnp.where(to // Y == zb, Z, zb)
        return remote(S.at[g, zb * Y + y], RZ.at[g, slot], rz_s.at[g, d, zb], rz_r.at[g, d, zb], {"mp": to})

    def zgot(g, d, zb, slot):
        to = me + Y if d == 0 else me - Y
        return remote(RZ.at[g, slot], RZ.at[g, slot], rz_s.at[g, d, zb], rz_r.at[g, d, zb], {"mp": to})

    def scatter_tasks(g):
        tasks = []

        def nth(t):
            if t == Z - 1:
                return z
            return jnp.where(z < Z // 2, Z - 1 - t - (Z - 1 - t <= z).astype(jnp.int32), t + (t >= z).astype(jnp.int32))

        def exchange(t):
            return ysum(g, nth(t), nth(t) * Y + 1 - y)

        def start():
            for t in range(min(FLIGHT, Z)):
                exchange(t).start()

        tasks.append(start)

        def pass_on(d, t):
            zb = Z - 1 - t + z if d == 0 else t - (Z - 1 - z)
            here = t >= z if d == 0 else t >= Z - 1 - z
            inner = has_dn if d == 0 else has_up

            @pl.when(here)
            def _():
                at = zb * Y + y
                ysum(g, zb, at).wait_recv()

                @pl.when(inner)
                def _():
                    zgot(g, d, zb, zb).wait_recv()
                    t = S[g, at].astype(jnp.float32) + Ry[g, zb].astype(jnp.float32)
                    S[g, at] = (t + RZ[g, zb].astype(jnp.float32)).astype(jnp.bfloat16)

                @pl.when(jnp.logical_not(inner))
                def _():
                    t = S[g, at].astype(jnp.float32) + Ry[g, zb].astype(jnp.float32)
                    S[g, at] = t.astype(jnp.bfloat16)

            send(here, functools.partial(zsum, g, d, zb))

        def advance(t):
            exchange(t).wait_send()
            if t + FLIGHT < Z:
                exchange(t + FLIGHT).start()

        for t in range(Z - 1):
            tasks.append(functools.partial(advance, t))
            for d in (0, 1):
                tasks.append(functools.partial(pass_on, d, t))
        tasks.append(functools.partial(advance, Z - 1))

        def finish():
            ysum(g, z, me).wait_recv()
            fsnd[g] = S[g, me].astype(jnp.float32) + Ry[g, z].astype(jnp.float32)

            @pl.when(has_dn)
            def _():
                zgot(g, 0, z, z).wait_recv()
                fsnd[g] += RZ[g, z].astype(jnp.float32)

            @pl.when(has_up)
            def _():
                zgot(g, 1, z, Z).wait_recv()
                fsnd[g] += RZ[g, Z].astype(jnp.float32)

            @pl.when(c == g)
            def _():
                columns = pl.ds(pl.multiple_of(c * H, H), H)
                out[:, columns] = (patches[:, columns].astype(jnp.float32) + fsnd[g]).astype(jnp.bfloat16)

            send(c != g, lambda: remote(fsnd.at[g], frecv, f_s, f_r, {"dp": o}))

        tasks.append(finish)
        return tasks

    def run(tasks):
        for t in tasks:
            t()

    first, second = gather_tasks(0), gather_tasks(1)
    late = 3
    run(first[:-late] + second[:1] + first[-late:])
    for w in wcopies:
        w.wait()
    run(weave(second[1:-late], compute_tasks(0)))
    lead, trail = scatter_tasks(0), scatter_tasks(1)
    run(lead[:1] + second[-late:])
    run(weave(lead[1:-late], compute_tasks(1)))
    run(trail[:1] + lead[-late:] + trail[1:])
    remote(fsnd.at[0], frecv, f_s, f_r, {"dp": o}).wait_recv()
    columns = pl.ds(pl.multiple_of(o * H, H), H)
    out[:, columns] = (patches[:, columns].astype(jnp.float32) + frecv[...]).astype(jnp.bfloat16)
    for cond, make in drains:
        if cond is None:
            make().wait_send()
        else:
            pl.when(cond)(lambda make=make: make().wait_send())


def shards(M, patches, norm_gain, query_gain, key_gain, joined_in, joined_out):
    R, D = patches.shape
    H = D // 2
    Z = M // Y
    G = M * R
    BW = joined_in.shape[2]
    BW2 = joined_out.shape[1]
    CW = 512
    NC = H // CW
    bf, f32 = jnp.bfloat16, jnp.float32
    V = pl.BlockSpec(memory_space=pltpu.VMEM)
    A = pl.BlockSpec(memory_space=pl.ANY)
    dma = pltpu.SemaphoreType.DMA
    return pl.pallas_call(
        functools.partial(kernel, M),
        out_shape=jax.ShapeDtypeStruct((R, D), bf),
        in_specs=[V, V, V, V, A, A],
        out_specs=V,
        scratch_shapes=[
            pltpu.VMEM((D, BW), bf),
            pltpu.VMEM((2, BW2, H), bf),
            pltpu.VMEM((2, 2, M, R, H), bf),
            pltpu.VMEM((G, BW), f32),
            pltpu.VMEM((G, BW2), bf),
            pltpu.VMEM((2, NC, G, CW), bf),
            pltpu.VMEM((2, NC, G, CW), bf),
            pltpu.VMEM((2, M, R, H), bf),
            pltpu.VMEM((2, Z, R, H), bf),
            pltpu.VMEM((2, Z + 1, R, H), bf),
            pltpu.VMEM((2, R, H), f32),
            pltpu.VMEM((R, H), f32),
            dma((6,)),
            dma((2,)), dma((2,)),
            dma((2, 2, Z)), dma((2, 2, Z)),
            dma((2, Z)), dma((2, Z)),
            dma((2, M)), dma((2, M)),
            dma((2, NC)), dma((2, NC)),
            dma((2, Z)), dma((2, Z)),
            dma((2, 2, Z)), dma((2, 2, Z)),
            dma, dma,
        ],
        compiler_params=pltpu.CompilerParams(
            collective_id=0, has_side_effects=True, vmem_limit_bytes=63 * 1024 * 1024
        ),
        cost_estimate=pl.CostEstimate(
            flops=4 * G * D * (BW + BW2), bytes_accessed=2 * D * (BW + BW2), transcendentals=0
        ),
    )(
        patches,
        norm_gain.reshape(1, -1),
        query_gain.reshape(1, -1),
        key_gain.reshape(1, -1),
        joined_in.reshape(D, BW),
        joined_out.reshape(BW2, D),
    )


def solution(mesh):
    in_specs = (
        P(("parts", "dp", "mp"), None),
        P(),
        P(),
        P(),
        P(None, ("dp", "mp"), None),
        P(("dp", "mp"), None, None),
    )
    out_specs = P(("parts", "dp", "mp"), None)
    body = functools.partial(shards, mesh.shape["mp"])
    return jax.shard_map(body, mesh=mesh, in_specs=in_specs, out_specs=out_specs, check_vma=False)
```
